32 devices in a mesh: groups: 2 (over y), ctx: 4 (over z), head: 2 (over x), rep: 2 (over core).
Axes of the slice: x: 2, y: 2, z: 4, core: 2. Of those that a mesh axis runs over, the one named last changes fastest.
Arguments:
- query_in: bfloat16 [4, 1024, 32, 128], P(('groups', 'rep'), 'ctx', 'head'), parts along dimension 0, may hold values from -6 to 6
- key_in: bfloat16 [4, 1024, 32, 128], P(('groups', 'rep'), 'ctx', 'head'), parts along dimension 0, may hold values from -6 to 6
- value_in: bfloat16 [4, 1024, 32, 128], P(('groups', 'rep'), 'ctx', 'head'), parts along dimension 0, may hold values from -6 to 6
- grad_out: bfloat16 [4, 1024, 32, 128], P(('groups', 'rep'), 'ctx', 'head'), parts along dimension 0, may hold values from -6 to 6
Outputs:
- output: bfloat16 [4, 1024, 32, 128], P(('groups', 'rep'), 'ctx', 'head'), parts along dimension 0
- grad_query: bfloat16 [4, 1024, 32, 128], P(('groups', 'rep'), 'ctx', 'head'), parts along dimension 0
- grad_key: bfloat16 [4, 1024, 32, 128], P(('groups', 'rep'), 'ctx', 'head'), parts along dimension 0
- grad_value: bfloat16 [4, 1024, 32, 128], P(('groups', 'rep'), 'ctx', 'head'), parts along dimension 0
The draws below stay inside these ranges and needn't reach their ends.
There are 2 independent parts, one for each index of `groups`. The reference program is written for one: setup_inputs(seed, part) draws one part's arguments, and reference() takes and returns one part's arrays. A program takes and returns all parts, laid end to end along the dimension named above; each array names one. Nothing has to cross between parts.
All inputs are finite; a program needn't handle non-finite values.
Results may differ from the reference program's by a relative error of at most 0.0073.
Values may be sent and summed in bfloat16 or wider, within the bound.
No kernel may reach another device: no remote copies, remote signals or barrier semaphores. Data moves between devices by JAX's collectives and lax.ppermute only.
A program may use at most 64 MiB of HBM per device.

```python
import jax
import jax.numpy as jnp
from jax import lax

HEADS = 32
DH = 128
SPAN = 256
SEQS = 2
LENGTH = 1024
N_CTX = 4


def levels(key, shape, shards, smallest, largest):
    loudness, own = 1.0, jax.random.fold_in(key, 6)
    for axis_at, blocks in shards:
        steps = jnp.exp(jax.random.uniform(jax.random.fold_in(own, axis_at), (blocks,), jnp.float32, smallest / len(shards), largest / len(shards)))
        loudness = loudness * jnp.repeat(steps, shape[axis_at] // blocks).reshape([-1 if axis == axis_at else 1 for axis in range(len(shape))])
    return loudness


def noise(own_key, shape, spread, most, cuts=(), held_as=jnp.bfloat16):
    drawn = jax.random.normal(own_key, shape, jnp.float32) * spread
    if len(cuts) > 0:
        drawn = levels(own_key, shape, cuts, -0.22, 0.18) * drawn
    return jnp.clip(drawn, min=-most, max=most).astype(held_as)


def setup_inputs(seed: int = 0, part: int = 0) -> dict:
    seeds = jax.random.split(jax.random.key(seed), 5)
    part_keys = jax.random.split(jax.random.fold_in(seeds[4], part), 5)
    return {
        "query_in": noise(part_keys[0], (SEQS, LENGTH, HEADS, DH), 1.0, 6.0, ((0, 2), (1, 4), (2, 2))),
        "key_in": noise(part_keys[1], (SEQS, LENGTH, HEADS, DH), 1.0, 6.0, ((0, 2), (1, 4), (2, 2))),
        "value_in": noise(part_keys[2], (SEQS, LENGTH, HEADS, DH), 1.0, 6.0, ((0, 2), (1, 4), (2, 2))),
        "grad_out": noise(part_keys[3], (SEQS, LENGTH, HEADS, DH), 1.0, 6.0, ((0, 2), (1, 4), (2, 2))),
    }


def silu_parts(raw_in):
    values = raw_in.astype(jnp.float32)
    sigma = jax.nn.sigmoid(values)
    return (values * sigma, sigma * (1.0 + values * (1.0 - sigma)))

def lower_mask(length):
    rows_idx = lax.broadcasted_iota(jnp.int32, (length, length), 0)
    cols_idx = lax.broadcasted_iota(jnp.int32, (length, length), 1)
    return rows_idx >= cols_idx

def block_state(pieces):
    query_blk, key_blk, value_blk, grad_blk = pieces
    feat_key = silu_parts(key_blk)[0].astype(jnp.bfloat16)
    return jnp.einsum('bshd,bshe->bhde', feat_key.astype(jnp.float32), value_blk.astype(jnp.float32))

def block_forward(pieces):
    query_blk, key_blk, value_blk, grad_blk, earlier = pieces
    feat_query = silu_parts(query_blk)[0].astype(jnp.bfloat16).astype(jnp.float32)
    feat_key = silu_parts(key_blk)[0].astype(jnp.bfloat16).astype(jnp.float32)
    values = value_blk.astype(jnp.float32)
    earlier_b = earlier.astype(jnp.bfloat16).astype(jnp.float32)
    mask_low = lower_mask(query_blk.shape[1])
    scores = jnp.einsum('bthd,bshd->bhts', feat_query, feat_key)
    scores = jnp.where(mask_low, scores, 0.0).astype(jnp.bfloat16).astype(jnp.float32)
    raw = jnp.einsum('bhts,bshd->bthd', scores, values) + jnp.einsum('bthd,bhde->bthe', feat_query, earlier_b)
    inverse = lax.rsqrt(lax.optimization_barrier(jnp.mean(raw * raw, axis=-1, keepdims=True)) + 1.0)
    normed = raw * inverse
    upstream = grad_blk.astype(jnp.float32)
    grad_raw = inverse * (upstream - normed * lax.optimization_barrier(jnp.mean(upstream * normed, axis=-1, keepdims=True)))
    grad_raw_b = grad_raw.astype(jnp.bfloat16)
    local_grad = jnp.einsum('bthd,bthe->bhde', feat_query, grad_raw_b.astype(jnp.float32))
    return (normed.astype(jnp.bfloat16), grad_raw_b, local_grad)

def block_backward(pieces):
    query_blk, key_blk, value_blk, grad_raw_b, earlier, later = pieces
    feat_query, slope_query = silu_parts(query_blk)
    feat_key, slope_key = silu_parts(key_blk)
    feat_query = feat_query.astype(jnp.bfloat16).astype(jnp.float32)
    feat_key = feat_key.astype(jnp.bfloat16).astype(jnp.float32)
    values = value_blk.astype(jnp.float32)
    grad_raw = grad_raw_b.astype(jnp.float32)
    earlier_b = earlier.astype(jnp.bfloat16).astype(jnp.float32)
    later_b = later.astype(jnp.bfloat16).astype(jnp.float32)
    mask_low = lower_mask(query_blk.shape[1])
    scores = jnp.einsum('bthd,bshd->bhts', feat_query, feat_key)
    scores = jnp.where(mask_low, scores, 0.0).astype(jnp.bfloat16).astype(jnp.float32)
    grad_scores = jnp.einsum('bthe,bshe->bhts', grad_raw, values)
    grad_scores = jnp.where(mask_low, grad_scores, 0.0).astype(jnp.bfloat16).astype(jnp.float32)
    grad_fq = jnp.einsum('bhts,bshd->bthd', grad_scores, feat_key) + jnp.einsum('bthe,bhde->bthd', grad_raw, earlier_b)
    grad_fk = jnp.einsum('bhts,bthd->bshd', grad_scores, feat_query) + jnp.einsum('bshe,bhde->bshd', values, later_b)
    grad_val = jnp.einsum('bhts,bthe->bshe', scores, grad_raw) + jnp.einsum('bshd,bhde->bshe', feat_key, later_b)
    return ((grad_fq * slope_query).astype(jnp.bfloat16), (grad_fk * slope_key).astype(jnp.bfloat16), grad_val.astype(jnp.bfloat16))

def split_blocks(array):
    shaped = array.reshape(SEQS, N_CTX, SPAN, HEADS, DH)
    return jnp.moveaxis(shaped, 1, 0)

def join_blocks(array):
    return jnp.moveaxis(array, 0, 1).reshape(SEQS, N_CTX * SPAN, HEADS, DH)

def reference(query_in, key_in, value_in, grad_out):
    query_bl = split_blocks(query_in)
    key_bl = split_blocks(key_in)
    value_bl = split_blocks(value_in)
    grad_bl = split_blocks(grad_out)
    local_state = lax.map(block_state, (query_bl, key_bl, value_bl, grad_bl))
    earlier = jnp.cumsum(local_state, axis=0) - local_state
    output, grad_raw_b, local_grad = lax.map(block_forward, (query_bl, key_bl, value_bl, grad_bl, earlier))
    later = jnp.cumsum(local_grad[::-1], axis=0)[::-1] - local_grad
    grad_query, grad_key, grad_value = lax.map(block_backward, (query_bl, key_bl, value_bl, grad_raw_b, earlier, later))
    return (join_blocks(output), join_blocks(grad_query), join_blocks(grad_key), join_blocks(grad_value))
```

```python
import functools

import jax
import jax.numpy as jnp
from jax import lax
from jax.experimental import pallas as pl
from jax.experimental.pallas import tpu as pltpu
from jax.sharding import PartitionSpec as P

BF, F32 = jnp.bfloat16, jnp.float32
MIB = 1 << 20
CHUNKS = 4


def dot(a, b, ca, cb):
    return lax.dot_general(a, b, (((ca,), (cb,)), ((), ())), preferred_element_type=F32)


def silu_parts(x):
    sigma = 1.0 / (1.0 + jnp.exp(-x))
    return x * sigma, sigma * (1.0 + x * (1.0 - sigma))


def low_mask(t):
    rows = lax.broadcasted_iota(jnp.int32, (t, t), 0)
    cols = lax.broadcasted_iota(jnp.int32, (t, t), 1)
    return rows >= cols


def widen(src, dst):
    dst[...] = src[...].astype(F32)


def key_kernel(heads, t, sizes, k_ref, v_ref, fk_ref, vh_ref, slope_ref, *rest):
    states, (k32, v32) = rest[: len(sizes)], rest[len(sizes) :]
    widen(k_ref, k32)
    widen(v_ref, v32)
    base = 0
    for state_ref, size in zip(states, sizes):

        def one(i, carry, base=base, state_ref=state_ref):
            h = base + i
            kh = k32[pl.ds(h, t, stride=heads), :]
            feat, slope = silu_parts(kh)
            feat = feat.astype(BF)
            vh = v32[pl.ds(h, t, stride=heads), :].astype(BF)
            fk_ref[h] = feat
            vh_ref[h] = vh
            slope_ref[h] = slope
            state_ref[i] = dot(feat, vh, 0, 0).astype(BF)
            return carry

        lax.fori_loop(0, size, one, 0)
        base += size


def query_kernel(heads, t, q_ref, g_ref, fk_ref, vh_ref, fq_ref, gh_ref, slope_ref, score_ref, raw_ref, q32, g32):
    widen(q_ref, q32)
    widen(g_ref, g32)

    def one(h, carry):
        qh = q32[pl.ds(h, t, stride=heads), :]
        feat, slope = silu_parts(qh)
        feat = feat.astype(BF)
        fq_ref[h] = feat
        slope_ref[h] = slope
        gh_ref[h] = g32[pl.ds(h, t, stride=heads), :].astype(BF)
        scores = jnp.where(low_mask(t), dot(feat, fk_ref[h], 1, 1), 0.0).astype(BF)
        score_ref[h] = scores
        raw_ref[h] = dot(scores, vh_ref[h], 1, 0)
        return carry

    lax.fori_loop(0, heads, one, 0)


def norm_kernel(base, size, parts, fq_ref, gh_ref, raw_ref, *rest):
    got, (normed_ref, grad_raw_ref, earlier_ref, grad_ref) = rest[:parts], rest[parts:]

    def one(i, carry):
        h = base + i
        earlier = got[0][i].astype(F32)
        for part in got[1:]:
            earlier = earlier + part[i].astype(F32)
        earlier = earlier.astype(BF)
        earlier_ref[i] = earlier
        fq = fq_ref[h]
        raw = raw_ref[h] + dot(fq, earlier, 1, 0)
        inverse = lax.rsqrt(jnp.mean(raw * raw, axis=-1, keepdims=True) + 1.0)
        normed = raw * inverse
        up = gh_ref[h].astype(F32)
        grad = inverse * (up - normed * jnp.mean(up * normed, axis=-1, keepdims=True))
        grad = grad.astype(BF)
        normed_ref[i] = normed.astype(BF)
        grad_raw_ref[i] = grad
        grad_ref[i] = dot(fq, grad, 0, 0).astype(BF)
        return carry

    lax.fori_loop(0, size, one, 0)


def back_kernel(base, size, t, fq_ref, fk_ref, vh_ref, slope_ref, score_ref, grad_raw_ref, earlier_ref, gq_ref, gk_ref, gv_ref):
    def one(i, carry):
        h = base + i
        grad = grad_raw_ref[i]
        fq = fq_ref[h]
        grad_scores = jnp.where(low_mask(t), dot(grad, vh_ref[h], 1, 1), 0.0).astype(BF)
        gfq = dot(grad_scores, fk_ref[h], 1, 0) + dot(grad, earlier_ref[i], 1, 1)
        gq_ref[i] = (gfq * slope_ref[h]).astype(BF)
        gk_ref[i] = dot(grad_scores, fq, 0, 0)
        gv_ref[i] = dot(score_ref[h], grad, 0, 0)
        return carry

    lax.fori_loop(0, size, one, 0)


def gather_kernel(heads, t, sizes, count, *refs):
    ins, outs, scratch = refs[: count * len(sizes)], refs[count * len(sizes) : -1], refs[-1]
    for a in range(count):
        base = 0
        for c, size in enumerate(sizes):
            piece = ins[a * len(sizes) + c]

            def one(i, carry, base=base, piece=piece):
                scratch[pl.ds(base + i, t, stride=heads), :] = piece[i].astype(F32)
                return carry

            lax.fori_loop(0, size, one, 0)
            base += size
        outs[a][...] = scratch[...].astype(BF)


def last_kernel(heads, t, sizes, parts, fk_ref, vh_ref, slope_ref, *refs):
    m = len(sizes)
    gks, gvs, refs = refs[:m], refs[m : 2 * m], refs[2 * m :]
    got, (gk_ref, gv_ref, k32, v32) = refs[: parts * m], refs[parts * m :]
    base = 0
    for c, size in enumerate(sizes):
        mine = got[c * parts : (c + 1) * parts]

        def one(i, carry, base=base, mine=mine, gk=gks[c], gv=gvs[c]):
            h = base + i
            later = mine[0][i].astype(F32)
            for part in mine[1:]:
                later = later + part[i].astype(F32)
            later = later.astype(BF)
            gfk = gk[i] + dot(vh_ref[h], later, 1, 1)
            k32[pl.ds(h, t, stride=heads), :] = gfk * slope_ref[h]
            v32[pl.ds(h, t, stride=heads), :] = gv[i] + dot(fk_ref[h], later, 1, 0)
            return carry

        lax.fori_loop(0, size, one, 0)
        base += size
    gk_ref[...] = k32[...].astype(BF)
    gv_ref[...] = v32[...].astype(BF)


def call(body, outs, scratch, args, flops, name):
    moved = sum(a.size * a.dtype.itemsize for a in args)
    return pl.pallas_call(
        body,
        out_shape=outs,
        scratch_shapes=scratch,
        compiler_params=pltpu.CompilerParams(vmem_limit_bytes=40 * MIB),
        cost_estimate=pl.CostEstimate(flops=flops, bytes_accessed=moved, transcendentals=0),
        name=name,
    )(*args)


def chain(part, n, reverse):
    got = []
    running = part
    for hop in range(n - 1):
        pair = (n - 1 - hop, n - 2 - hop) if reverse else (hop, hop + 1)
        received = lax.ppermute(running, "ctx", [pair])
        got.append(received)
        running = (part.astype(F32) + received.astype(F32)).astype(BF)
    return got


def shards(n, query_in, key_in, value_in, grad_out):
    _, t, heads, d = query_in.shape
    m = min(CHUNKS, heads)
    sizes = [heads // m + (1 if c < heads % m else 0) for c in range(m)]
    bases = [sum(sizes[:c]) for c in range(m)]
    q, k, v, g = (a.reshape(t * heads, d) for a in (query_in, key_in, value_in, grad_out))
    S = jax.ShapeDtypeStruct
    whole = lambda dt: S((heads, t, d), dt)
    flat = S((t * heads, d), BF)
    wide = pltpu.VMEM((t * heads, d), F32)
    mm = 2 * t * d * d

    fk, vh, slope_k, *states = call(
        functools.partial(key_kernel, heads, t, sizes),
        [whole(BF), whole(BF), whole(F32)] + [S((s, d, d), BF) for s in sizes],
        [wide, wide], (k, v), heads * mm, "key",
    )
    ups = [chain(s, n, False) for s in states]
    fq, gh, slope_q, scores, raw = call(
        functools.partial(query_kernel, heads, t),
        [whole(BF), whole(BF), whole(F32), S((heads, t, t), BF), whole(F32)],
        [wide, wide], (q, g, fk, vh), heads * mm * 4, "query",
    )
    normed, gqs, gks, gvs, downs = [], [], [], [], []
    for c in range(m):
        s = sizes[c]
        piece = lambda dt: S((s, t, d), dt)
        nb, grad_raw, earlier, grad = call(
            functools.partial(norm_kernel, bases[c], s, n - 1),
            [piece(BF), piece(BF), S((s, d, d), BF), S((s, d, d), BF)],
            [], (fq, gh, raw, *ups[c]), s * mm * 2, "norm",
        )
        normed.append(nb)
        downs.append(chain(grad, n, True))
        gq, gk, gv = call(
            functools.partial(back_kernel, bases[c], s, t),
            [piece(BF), piece(F32), piece(F32)],
            [], (fq, fk, vh, slope_q, scores, grad_raw, earlier), s * mm * 9, "back",
        )
        gqs.append(gq)
        gks.append(gk)
        gvs.append(gv)
    output, grad_query = call(
        functools.partial(gather_kernel, heads, t, sizes, 2),
        [flat, flat], [wide], (*normed, *gqs), heads * mm, "gather",
    )
    grad_key, grad_value = call(
        functools.partial(last_kernel, heads, t, sizes, n - 1),
        [flat, flat], [wide, wide],
        (fk, vh, slope_k, *gks, *gvs, *[r for down in downs for r in down]), heads * mm * 2, "last",
    )
    return tuple(a.reshape(1, t, heads, d) for a in (output, grad_query, grad_key, grad_value))


def solution(mesh):
    placed = P(("groups", "rep"), "ctx", "head", None)
    return jax.shard_map(
        functools.partial(shards, mesh.shape["ctx"]),
        mesh=mesh,
        in_specs=(placed,) * 4,
        out_specs=(placed,) * 4,
        check_vma=False,
    )
```

```python
import functools

import jax
import jax.numpy as jnp
from jax import lax
from jax.experimental import pallas as pl
from jax.experimental.pallas import tpu as pltpu
from jax.sharding import PartitionSpec as P

BF, F32 = jnp.bfloat16, jnp.float32
MIB = 1 << 20
CHUNKS = 4
UNROLL = 4


def dot(a, b, ca, cb):
    return lax.dot_general(a, b, (((ca,), (cb,)), ((), ())), preferred_element_type=F32)


def silu_parts(x):
    sigma = 1.0 / (1.0 + jnp.exp(-x))
    return x * sigma, sigma * (1.0 + x * (1.0 - sigma))


def low_mask(t):
    rows = lax.broadcasted_iota(jnp.int32, (t, t), 0)
    cols = lax.broadcasted_iota(jnp.int32, (t, t), 1)
    return rows >= cols


def widen(src, dst):
    dst[...] = src[...].astype(F32)


def key_kernel(heads, t, sizes, k_ref, v_ref, fk_ref, vh_ref, slope_ref, *rest):
    states, (k32, v32) = rest[: len(sizes)], rest[len(sizes) :]
    widen(k_ref, k32)
    widen(v_ref, v32)
    base = 0
    for state_ref, size in zip(states, sizes):

        def one(i, carry, base=base, state_ref=state_ref):
            h = base + i
            kh = k32[pl.ds(h, t, stride=heads), :]
            feat, slope = silu_parts(kh)
            feat = feat.astype(BF)
            vh = v32[pl.ds(h, t, stride=heads), :].astype(BF)
            fk_ref[h] = feat
            vh_ref[h] = vh
            slope_ref[h] = slope
            state_ref[i] = dot(feat, vh, 0, 0).astype(BF)
            return carry

        lax.fori_loop(0, size, one, 0, unroll=UNROLL)
        base += size


def query_kernel(heads, t, q_ref, g_ref, fk_ref, vh_ref, fq_ref, gh_ref, slope_ref, score_ref, raw_ref, q32, g32):
    widen(q_ref, q32)
    widen(g_ref, g32)

    def one(h, carry):
        qh = q32[pl.ds(h, t, stride=heads), :]
        feat, slope = silu_parts(qh)
        feat = feat.astype(BF)
        fq_ref[h] = feat
        slope_ref[h] = slope
        gh_ref[h] = g32[pl.ds(h, t, stride=heads), :].astype(BF)
        scores = jnp.where(low_mask(t), dot(feat, fk_ref[h], 1, 1), 0.0).astype(BF)
        score_ref[h] = scores
        raw_ref[h] = dot(scores, vh_ref[h], 1, 0)
        return carry

    lax.fori_loop(0, heads, one, 0, unroll=UNROLL)


def norm_kernel(base, size, parts, fq_ref, gh_ref, raw_ref, *rest):
    got, (normed_ref, grad_raw_ref, earlier_ref, grad_ref) = rest[:parts], rest[parts:]

    def one(i, carry):
        h = base + i
        earlier = pick(lax.axis_index("ctx"), got, i)
        earlier_ref[i] = earlier
        fq = fq_ref[h]
        raw = raw_ref[h] + dot(fq, earlier, 1, 0)
        inverse = lax.rsqrt(jnp.mean(raw * raw, axis=-1, keepdims=True) + 1.0)
        normed = raw * inverse
        up = gh_ref[h].astype(F32)
        grad = inverse * (up - normed * jnp.mean(up * normed, axis=-1, keepdims=True))
        grad = grad.astype(BF)
        normed_ref[i] = normed.astype(BF)
        grad_raw_ref[i] = grad
        grad_ref[i] = dot(fq, grad, 0, 0).astype(BF)
        return carry

    lax.fori_loop(0, size, one, 0, unroll=UNROLL)


def back_kernel(base, size, t, fq_ref, fk_ref, vh_ref, slope_ref, score_ref, grad_raw_ref, earlier_ref, gq_ref, gk_ref, gv_ref):
    def one(i, carry):
        h = base + i
        grad = grad_raw_ref[i]
        fq = fq_ref[h]
        grad_scores = jnp.where(low_mask(t), dot(grad, vh_ref[h], 1, 1), 0.0).astype(BF)
        gfq = dot(grad_scores, fk_ref[h], 1, 0) + dot(grad, earlier_ref[i], 1, 1)
        gq_ref[i] = (gfq * slope_ref[h]).astype(BF)
        gk_ref[i] = dot(grad_scores, fq, 0, 0)
        gv_ref[i] = dot(score_ref[h], grad, 0, 0)
        return carry

    lax.fori_loop(0, size, one, 0, unroll=UNROLL)


def gather_kernel(heads, t, sizes, count, *refs):
    ins, outs, scratch = refs[: count * len(sizes)], refs[count * len(sizes) : -1], refs[-1]
    for a in range(count):
        base = 0
        for c, size in enumerate(sizes):
            piece = ins[a * len(sizes) + c]

            def one(i, carry, base=base, piece=piece):
                scratch[pl.ds(base + i, t, stride=heads), :] = piece[i].astype(F32)
                return carry

            lax.fori_loop(0, size, one, 0, unroll=UNROLL)
            base += size
        outs[a][...] = scratch[...].astype(BF)


def last_kernel(heads, t, sizes, parts, fk_ref, vh_ref, slope_ref, *refs):
    m = len(sizes)
    gks, gvs, refs = refs[:m], refs[m : 2 * m], refs[2 * m :]
    got, (gk_ref, gv_ref, k32, v32) = refs[: parts * m], refs[parts * m :]
    base = 0
    for c, size in enumerate(sizes):
        mine = got[c * parts : (c + 1) * parts]

        def one(i, carry, base=base, mine=mine, gk=gks[c], gv=gvs[c]):
            h = base + i
            later = pick(parts - lax.axis_index("ctx"), mine, i)
            gfk = gk[i] + dot(vh_ref[h], later, 1, 1)
            k32[pl.ds(h, t, stride=heads), :] = gfk * slope_ref[h]
            v32[pl.ds(h, t, stride=heads), :] = gv[i] + dot(fk_ref[h], later, 1, 0)
            return carry

        lax.fori_loop(0, size, one, 0, unroll=UNROLL)
        base += size
    gk_ref[...] = k32[...].astype(BF)
    gv_ref[...] = v32[...].astype(BF)


def call(body, outs, scratch, args, flops, name):
    moved = sum(a.size * a.dtype.itemsize for a in args)
    return pl.pallas_call(
        body,
        out_shape=outs,
        scratch_shapes=scratch,
        compiler_params=pltpu.CompilerParams(vmem_limit_bytes=40 * MIB),
        cost_estimate=pl.CostEstimate(flops=flops, bytes_accessed=moved, transcendentals=0),
        name=name,
    )(*args)


def swap(x, low, n, cores):
    pairs = []
    for c in range(n):
        for r in range(cores):
            to = (2 * low + 1 - c, r) if c in (low, low + 1) else (c, r ^ 1 if cores % 2 == 0 else r)
            pairs.append((c * cores + r, to[0] * cores + to[1]))
    return lax.ppermute(x, ("ctx", "rep"), pairs)


def chain(part, n, cores, reverse):
    got = []
    running = part
    for hop in range(n - 1):
        received = swap(running, n - 2 - hop if reverse else hop, n, cores)
        got.append(received)
        running = (part.astype(F32) + received.astype(F32)).astype(BF)
    return got


def pick(place, got, i):
    total = jnp.zeros(got[0].shape[1:], got[0].dtype)
    for hop, part in enumerate(got):
        total = jnp.where(place == hop + 1, part[i], total)
    return total


def shards(n, cores, query_in, key_in, value_in, grad_out):
    _, t, heads, d = query_in.shape
    m = min(CHUNKS, heads)
    sizes = [heads // m + (1 if c < heads % m else 0) for c in range(m)]
    bases = [sum(sizes[:c]) for c in range(m)]
    q, k, v, g = (a.reshape(t * heads, d) for a in (query_in, key_in, value_in, grad_out))
    S = jax.ShapeDtypeStruct
    whole = lambda dt: S((heads, t, d), dt)
    flat = S((t * heads, d), BF)
    wide = pltpu.VMEM((t * heads, d), F32)
    mm = 2 * t * d * d

    fk, vh, slope_k, *states = call(
        functools.partial(key_kernel, heads, t, sizes),
        [whole(BF), whole(BF), whole(F32)] + [S((s, d, d), BF) for s in sizes],
        [wide, wide], (k, v), heads * mm, "key",
    )
    ups = [chain(s, n, cores, False) for s in states]
    fq, gh, slope_q, scores, raw = call(
        functools.partial(query_kernel, heads, t),
        [whole(BF), whole(BF), whole(F32), S((heads, t, t), BF), whole(F32)],
        [wide, wide], (q, g, fk, vh), heads * mm * 4, "query",
    )
    normed, gqs, gks, gvs, downs = [], [], [], [], []
    for c in range(m):
        s = sizes[c]
        piece = lambda dt: S((s, t, d), dt)
        nb, grad_raw, earlier, grad = call(
            functools.partial(norm_kernel, bases[c], s, n - 1),
            [piece(BF), piece(BF), S((s, d, d), BF), S((s, d, d), BF)],
            [], (fq, gh, raw, *ups[c]), s * mm * 2, "norm",
        )
        normed.append(nb)
        downs.append(chain(grad, n, cores, True))
        gq, gk, gv = call(
            functools.partial(back_kernel, bases[c], s, t),
            [piece(BF), piece(F32), piece(F32)],
            [], (fq, fk, vh, slope_q, scores, grad_raw, earlier), s * mm * 9, "back",
        )
        gqs.append(gq)
        gks.append(gk)
        gvs.append(gv)
    output, grad_query = call(
        functools.partial(gather_kernel, heads, t, sizes, 2),
        [flat, flat], [wide], (*normed, *gqs), heads * mm, "gather",
    )
    grad_key, grad_value = call(
        functools.partial(last_kernel, heads, t, sizes, n - 1),
        [flat, flat], [wide, wide],
        (fk, vh, slope_k, *gks, *gvs, *[r for down in downs for r in down]), heads * mm * 2, "last",
    )
    return tuple(a.reshape(1, t, heads, d) for a in (output, grad_query, grad_key, grad_value))


def solution(mesh):
    placed = P(("groups", "rep"), "ctx", "head", None)
    return jax.shard_map(
        functools.partial(shards, mesh.shape["ctx"], mesh.shape["rep"]),
        mesh=mesh,
        in_specs=(placed,) * 4,
        out_specs=(placed,) * 4,
        check_vma=False,
    )
```

```python
import functools

import jax
import jax.numpy as jnp
from jax import lax
from jax.experimental import pallas as pl
from jax.experimental.pallas import tpu as pltpu
from jax.sharding import PartitionSpec as P

BF, F32 = jnp.bfloat16, jnp.float32
MIB = 1 << 20
SIZES = [4, 4, 4, 4]
UNROLL = 4
BLOCKS = 4


def dot(a, b, ca, cb):
    return lax.dot_general(a, b, (((ca,), (cb,)), ((), ())), preferred_element_type=F32)


def silu_parts(x):
    sigma = 1.0 / (1.0 + jnp.exp(-x))
    return x * sigma, sigma * (1.0 + x * (1.0 - sigma))


def low_mask(t):
    rows = lax.broadcasted_iota(jnp.int32, (t, t), 0)
    cols = lax.broadcasted_iota(jnp.int32, (t, t), 1)
    return rows >= cols


def widen(src, dst):
    dst[...] = src[...].astype(F32)


def blocks_of(rows):
    size = rows // BLOCKS if rows % (16 * BLOCKS) == 0 else rows
    return [pl.ds(at, size) for at in range(0, rows, size)]


def fetch(sources, landings, wides, sems):
    copies = []
    for src, dst, wide in zip(sources, landings, wides):
        for rows in blocks_of(src.shape[0]):
            copy = pltpu.make_async_copy(src.at[rows], dst.at[rows], sems.at[len(copies)])
            copy.start()
            copies.append((copy, dst, wide, rows))
    for copy, dst, wide, rows in copies:
        copy.wait()
        wide[rows, :] = dst[rows, :].astype(F32)


def flush(wides, stages, results, sems):
    copies = []
    for wide, stage, dst in zip(wides, stages, results):
        for rows in blocks_of(wide.shape[0]):
            stage[rows, :] = wide[rows, :].astype(BF)
            copies.append(pltpu.make_async_copy(stage.at[rows], dst.at[rows], sems.at[len(copies)]))
            copies[-1].start()
    for copy in copies:
        copy.wait()


def key_kernel(base, size, heads, t, first, *refs):
    if first:
        k_ref, v_ref, state_ref, fk_ref, vh_ref, slope_ref, k32, v32, k16, v16, sems = refs
        fetch((k_ref, v_ref), (k16, v16), (k32, v32), sems)
    else:
        k32, v32, state_ref, fk_ref, vh_ref, slope_ref = refs

    def one(i, carry):
        feat, slope = silu_parts(k32[pl.ds(base + i, t, stride=heads), :])
        feat = feat.astype(BF)
        vh = v32[pl.ds(base + i, t, stride=heads), :].astype(BF)
        fk_ref[i] = feat
        vh_ref[i] = vh
        slope_ref[i] = slope
        state_ref[i] = dot(feat, vh, 0, 0).astype(BF)
        return carry

    lax.fori_loop(0, size, one, 0, unroll=UNROLL)


def query_kernel(base, size, heads, t, first, *refs):
    if first:
        q_ref, g_ref, fk_ref, vh_ref, raw_ref, fq_ref, gh_ref, slope_ref, score_ref, q32, g32 = refs
        widen(q_ref, q32)
        widen(g_ref, g32)
    else:
        q32, g32, fk_ref, vh_ref, raw_ref, fq_ref, gh_ref, slope_ref, score_ref = refs

    def one(i, carry):
        feat, slope = silu_parts(q32[pl.ds(base + i, t, stride=heads), :])
        feat = feat.astype(BF)
        fq_ref[i] = feat
        slope_ref[i] = slope
        gh_ref[i] = g32[pl.ds(base + i, t, stride=heads), :].astype(BF)
        scores = jnp.where(low_mask(t), dot(feat, fk_ref[i], 1, 1), 0.0).astype(BF)
        score_ref[i] = scores
        raw_ref[i] = dot(scores, vh_ref[i], 1, 0)
        return carry

    lax.fori_loop(0, size, one, 0, unroll=UNROLL)


def norm_kernel(base, size, heads, t, parts, fq_ref, gh_ref, raw_ref, *rest):
    got, (grad_ref, grad_raw_ref, earlier_ref, wide_ref) = rest[:parts], rest[-4:]

    def one(i, carry):
        earlier = pick(lax.axis_index("ctx"), got, i)
        earlier_ref[i] = earlier
        fq = fq_ref[i]
        raw = raw_ref[i] + dot(fq, earlier, 1, 0)
        inverse = lax.rsqrt(jnp.mean(raw * raw, axis=-1, keepdims=True) + 1.0)
        normed = raw * inverse
        up = gh_ref[i].astype(F32)
        grad = inverse * (up - normed * jnp.mean(up * normed, axis=-1, keepdims=True))
        grad = grad.astype(BF)
        wide_ref[pl.ds(base + i, t, stride=heads), :] = normed
        grad_raw_ref[i] = grad
        grad_ref[i] = dot(fq, grad, 0, 0).astype(BF)
        return carry

    lax.fori_loop(0, size, one, 0, unroll=UNROLL)


def back_kernel(base, size, heads, t, fq_ref, fk_ref, vh_ref, slope_ref, score_ref, grad_raw_ref, earlier_ref, *rest):
    gk_ref, gv_ref, wide_ref = rest[-3:]

    def one(i, carry):
        grad = grad_raw_ref[i]
        fq = fq_ref[i]
        grad_scores = jnp.where(low_mask(t), dot(grad, vh_ref[i], 1, 1), 0.0).astype(BF)
        gfq = dot(grad_scores, fk_ref[i], 1, 0) + dot(grad, earlier_ref[i], 1, 1)
        wide_ref[pl.ds(base + i, t, stride=heads), :] = gfq * slope_ref[i]
        gk_ref[i] = dot(grad_scores, fq, 0, 0)
        gv_ref[i] = dot(score_ref[i], grad, 0, 0)
        return carry

    lax.fori_loop(0, size, one, 0, unroll=UNROLL)


def gather_kernel(count, *refs):
    flush(refs[:count], refs[2 * count : 3 * count], refs[count : 2 * count], refs[-1])


def later_step(base, size, heads, t, parts, refs, wide_k, wide_v):
    fk_ref, vh_ref, slope_ref, gk, gv = refs[:5]
    got = refs[5 : 5 + parts]

    def one(i, carry):
        later = pick(parts - lax.axis_index("ctx"), got, i)
        gfk = gk[i] + dot(vh_ref[i], later, 1, 1)
        wide_k[pl.ds(base + i, t, stride=heads), :] = gfk * slope_ref[i]
        wide_v[pl.ds(base + i, t, stride=heads), :] = gv[i] + dot(fk_ref[i], later, 1, 0)
        return carry

    lax.fori_loop(0, size, one, 0, unroll=UNROLL)


def later_kernel(base, size, heads, t, parts, *refs):
    later_step(base, size, heads, t, parts, refs, *refs[-2:])


def last_kernel(base, size, heads, t, parts, *refs):
    if base:
        wide_k, wide_v, k_out, v_out, k16, v16, sems = refs[5 + parts :]
    else:
        k_out, v_out, k16, v16, sems, wide_k, wide_v = refs[5 + parts :]
    later_step(base, size, heads, t, parts, refs, wide_k, wide_v)
    flush((wide_k, wide_v), (k16, v16), (k_out, v_out), sems)


def call(body, outs, scratch, args, flops, name, specs, out_specs, aliases):
    moved = sum(a.size * a.dtype.itemsize for a in args)
    return pl.pallas_call(
        body,
        out_shape=outs,
        in_specs=specs,
        out_specs=out_specs,
        scratch_shapes=scratch,
        input_output_aliases=aliases,
        compiler_params=pltpu.CompilerParams(vmem_limit_bytes=28 * MIB),
        cost_estimate=pl.CostEstimate(flops=flops, bytes_accessed=moved, transcendentals=0),
        name=name,
    )(*args)


def swap(x, low, n, cores):
    pairs = []
    for c in range(n):
        for r in range(cores):
            to = (2 * low + 1 - c, r) if c in (low, low + 1) else (c, r ^ 1 if cores % 2 == 0 else r)
            pairs.append((c * cores + r, to[0] * cores + to[1]))
    return lax.ppermute(x, ("ctx", "rep"), pairs)


class Order:
    def __init__(self):
        self.before = []

    def tie(self, x):
        return lax.optimization_barrier((x, *self.before))[0] if self.before else x

    def compute(self, body, outs, scratch, args, tied, flops, name, far_in=(), far_out=(), aliases={}):
        args = list(args)
        args[tied] = self.tie(args[tied])
        for i in far_in:
            args[i] = pltpu.with_memory_space_constraint(args[i], pltpu.HBM)
        near, far = pl.BlockSpec(memory_space=pltpu.VMEM), pl.BlockSpec(memory_space=pltpu.HBM)
        made = call(
            body, outs, scratch, args, flops, name,
            [far if i in far_in else near for i in range(len(args))],
            [far if i in far_out else near for i in range(len(outs))], aliases,
        )
        self.before = [made[0]]
        return made


class Chain:
    def __init__(self, order, part, n, cores, reverse):
        self.order, self.part, self.n, self.cores, self.reverse = order, part, n, cores, reverse
        self.got = []

    def hop(self):
        h = len(self.got)
        if h:
            running = (self.part.astype(F32) + self.order.tie(self.got[-1]).astype(F32)).astype(BF)
        else:
            running = self.order.tie(self.part)
        self.order.before.append(running)
        self.got.append(swap(running, self.n - 2 - h if self.reverse else h, self.n, self.cores))


def pick(place, got, i):
    total = jnp.zeros(got[0].shape[1:], got[0].dtype)
    for hop, part in enumerate(got):
        total = jnp.where(place == hop + 1, part[i], total)
    return total


ORDER = [
    "k0", "u0", "k1", "u1", "q0", "k2", "u2", "k3", "u0", "u3", "q1", "u1", "u0", "u2",
    "q2", "u1", "u3", "u2", "n0", "d0", "n1", "d1", "q3", "b0", "u3", "n2", "d0", "b2",
    "d2", "d1", "n3", "d3", "d0", "b3", "d2", "d1", "g0", "d3", "d2", "b1", "d3", "g1",
    "l0", "l1", "l2", "l3",
]


def plan(hops):
    left = {step: ORDER.count(step) for step in ORDER}
    for step in ORDER:
        left[step] -= 1
        if step[0] not in "ud":
            yield step
            continue
        listed = ORDER.count(step)
        done = listed - left[step]
        if done <= hops:
            yield from [step] * (hops - listed + 1 if left[step] == 0 and hops > listed else 1)


def shards(n, cores, query_in, key_in, value_in, grad_out):
    _, t, heads, d = query_in.shape
    sizes = SIZES if sum(SIZES) == heads else [heads // len(SIZES)] * len(SIZES)
    assert sum(sizes) == heads
    m = len(sizes)
    bases = [sum(sizes[:c]) for c in range(m)]
    q, k, v, g = (a.reshape(t * heads, d) for a in (query_in, key_in, value_in, grad_out))
    S = jax.ShapeDtypeStruct
    flat = S((t * heads, d), BF)
    wide = pltpu.VMEM((t * heads, d), F32)
    mm = 2 * t * d * d

    order = Order()
    flat16 = pltpu.VMEM((t * heads, d), BF)
    sems = pltpu.SemaphoreType.DMA((2 * BLOCKS,))
    broad = S((t * heads, d), F32)
    up, down, parts, held = {}, {}, {}, {}

    def of(c, dt):
        return S((sizes[c], t, d), dt)

    def key(c):
        outs = [S((sizes[c], d, d), BF), of(c, BF), of(c, BF), of(c, F32)]
        body = functools.partial(key_kernel, bases[c], sizes[c], heads, t, c == 0)
        if c == 0:
            state, *held["key", c], held["k32"], held["v32"] = order.compute(
                body, outs + [broad] * 2, [flat16, flat16, sems], (k, v), 0, sizes[c] * mm, "key", far_in=(0, 1)
            )
        else:
            state, *held["key", c] = order.compute(
                body, outs, [], (held["k32"], held["v32"]), 0, sizes[c] * mm, "key"
            )
        up[c] = Chain(order, state, n, cores, False)

    def query(c):
        outs = [of(c, F32), of(c, BF), of(c, BF), of(c, F32), S((sizes[c], t, t), BF)]
        fk, vh, _ = held["key", c]
        body = functools.partial(query_kernel, bases[c], sizes[c], heads, t, c == 0)
        if c == 0:
            *held["query", c], held["q32"], held["g32"] = order.compute(
                body, outs + [broad] * 2, [], (q, g, fk, vh), 2, sizes[c] * mm * 4, "query"
            )
        else:
            held["query", c] = order.compute(
                body, outs, [], (held["q32"], held["g32"], fk, vh), 2, sizes[c] * mm * 4, "query"
            )

    def onto(args, outs, names):
        have = [held[name] for name in names if name in held]
        aliases = {len(args) + i: len(outs) + i for i in range(len(have))}
        return (*args, *have), outs + [broad] * len(names), aliases

    def norm(c):
        raw, fq, gh, _, _ = held["query", c]
        s = sizes[c]
        state = S((s, d, d), BF)
        args, outs, aliases = onto((fq, gh, raw, *up[c].got), [state, S((s, t, d), BF), state], ["normed"])
        grad, grad_raw, earlier, held["normed"] = order.compute(
            functools.partial(norm_kernel, bases[c], s, heads, t, n - 1),
            outs, [], args, 3, s * mm * 2, "norm", aliases=aliases,
        )
        held[c] = grad_raw, earlier
        down[c] = Chain(order, grad, n, cores, True)

    def back(c):
        _, fq, _, slope_q, scores = held["query", c]
        fk, vh, _ = held["key", c]
        s = sizes[c]
        piece = S((s, t, d), F32)
        args, outs, aliases = onto((fq, fk, vh, slope_q, scores, *held[c]), [piece, piece], ["gq"])
        *parts[c], held["gq"] = order.compute(
            functools.partial(back_kernel, bases[c], s, heads, t),
            outs, [], args, 6, s * mm * 9, "back", aliases=aliases,
        )

    def gather(which):
        name = ("normed", "gq")[which]
        held["out", which], = order.compute(
            functools.partial(gather_kernel, 1), [flat], [flat16, sems], [held[name]], 0, heads * mm, "gather",
            far_out=(0,),
        )

    def later(c):
        s = sizes[c]
        args = (*held["key", c], *parts[c], *down[c].got)
        if c < m - 1:
            args, outs, aliases = onto(args, [], ["gk", "gv"])
            held["gk"], held["gv"] = order.compute(
                functools.partial(later_kernel, bases[c], s, heads, t, n - 1),
                outs, [], args, 5, s * mm * 2, "later", aliases=aliases,
            )
        else:
            wides = [held["gk"], held["gv"]] if m > 1 else []
            held["last"] = order.compute(
                functools.partial(last_kernel, bases[c], s, heads, t, n - 1),
                [flat, flat], [flat16, flat16, sems] + ([] if wides else [wide, wide]),
                (*args, *wides), 5, s * mm * 2, "last", far_out=(0, 1),
            )

    steps = dict(
        u=lambda c: up[c].hop(), d=lambda c: down[c].hop(), k=key, q=query, n=norm, b=back, g=gather, l=later
    )
    for step in plan(n - 1):
        steps[step[0]](*map(int, step[1:].split(".") if step[1:] else ()))
    output, grad_query = held["out", 0], held["out", 1]
    grad_key, grad_value = held["last"]
    return tuple(a.reshape(1, t, heads, d) for a in (output, grad_query, grad_key, grad_value))


def solution(mesh):
    placed = P(("groups", "rep"), "ctx", "head", None)
    return jax.shard_map(
        functools.partial(shards, mesh.shape["ctx"], mesh.shape["rep"]),
        mesh=mesh,
        in_specs=(placed,) * 4,
        out_specs=(placed,) * 4,
        check_vma=False,
    )
```

```python
import functools

import jax
import jax.numpy as jnp
from jax import lax
from jax.experimental import pallas as pl
from jax.experimental.pallas import tpu as pltpu
from jax.sharding import PartitionSpec as P

BF, F32 = jnp.bfloat16, jnp.float32
MIB = 1 << 20
SCOPED = 12 * MIB
SIZES = [4, 4, 4, 4]
UNROLL = 4
BLOCKS = 4
ORDER = [
    "k0", "u0", "k1", "k3", "u1", "q0", "k2", "u2", "u0", "u3", "u1", "q3", "u0", "u2",
    "q1", "u1", "u3", "n0", "x20", "b0", "n1", "x31", "q2", "d0", "n2", "d2", "d1", "n3",
    "d3", "d0", "d2", "d1", "g0", "d3", "d2", "b3", "b1", "d3", "b2", "g1", "l1", "l0",
    "l2", "l3",
]


def dot(a, b, ca, cb):
    return lax.dot_general(a, b, (((ca,), (cb,)), ((), ())), preferred_element_type=F32)


def silu_parts(x):
    sigma = 1.0 / (1.0 + jnp.exp(-x))
    return x * sigma, sigma * (1.0 + x * (1.0 - sigma))


def low_mask(t):
    rows = lax.broadcasted_iota(jnp.int32, (t, t), 0)
    cols = lax.broadcasted_iota(jnp.int32, (t, t), 1)
    return rows >= cols


def widen(src, dst):
    dst[...] = src[...].astype(F32)


def blocks_of(rows):
    size = rows // BLOCKS if rows % (16 * BLOCKS) == 0 else rows
    return [pl.ds(at, size) for at in range(0, rows, size)]


def fetch(src, landing, sems):
    copies = []
    for rows in blocks_of(src.shape[0]):
        copies.append((pltpu.make_async_copy(src.at[rows], landing.at[rows], sems.at[len(copies)]), rows))
        copies[-1][0].start()
    return copies


def land(copies, landing, wide):
    for copy, rows in copies:
        copy.wait()
        wide[rows, :] = landing[rows, :].astype(F32)


def flush(wides, stages, results, sems):
    copies = []
    for wide, stage, dst in zip(wides, stages, results):
        for rows in blocks_of(wide.shape[0]):
            stage[rows, :] = wide[rows, :].astype(BF)
            copies.append(pltpu.make_async_copy(stage.at[rows], dst.at[rows], sems.at[len(copies)]))
            copies[-1].start()
    for copy in copies:
        copy.wait()


def key_kernel(base, size, heads, t, first, *refs):
    if first:
        k_ref, v_ref, state_ref, fk_ref, vh_ref, slope_ref, k32, v32, k16, v16, k_sems, v_sems = refs
        k_copies, v_copies = fetch(k_ref, k16, k_sems), fetch(v_ref, v16, v_sems)
        land(k_copies, k16, k32)
        land(v_copies, v16, v32)
    else:
        k32, v32, state_ref, fk_ref, vh_ref, slope_ref = refs

    def one(i, carry):
        feat, slope = silu_parts(k32[pl.ds(base + i, t, stride=heads), :])
        feat = feat.astype(BF)
        vh = v32[pl.ds(base + i, t, stride=heads), :].astype(BF)
        fk_ref[i] = feat
        vh_ref[i] = vh
        slope_ref[i] = slope
        state_ref[i] = dot(feat, vh, 0, 0).astype(BF)
        return carry

    lax.fori_loop(0, size, one, 0, unroll=UNROLL)


def query_kernel(base, size, heads, t, first, *refs):
    if first:
        q_ref, g_ref, fk_ref, vh_ref, raw_ref, fq_ref, gh_ref, slope_ref, score_ref, q32, g32 = refs
        widen(q_ref, q32)
        widen(g_ref, g32)
    else:
        q32, g32, fk_ref, vh_ref, raw_ref, fq_ref, gh_ref, slope_ref, score_ref = refs

    def one(i, carry):
        feat, slope = silu_parts(q32[pl.ds(base + i, t, stride=heads), :])
        feat = feat.astype(BF)
        fq_ref[i] = feat
        slope_ref[i] = slope
        gh_ref[i] = g32[pl.ds(base + i, t, stride=heads), :].astype(BF)
        scores = jnp.where(low_mask(t), dot(feat, fk_ref[i], 1, 1), 0.0).astype(BF)
        score_ref[i] = scores
        raw_ref[i] = dot(scores, vh_ref[i], 1, 0)
        return carry

    lax.fori_loop(0, size, one, 0, unroll=UNROLL)


def norm_kernel(base, size, heads, t, chain, fq_ref, gh_ref, raw_ref, *rest):
    got, (grad_ref, grad_raw_ref, earlier_ref, wide_ref) = rest[: chain.hops], rest[-4:]

    def one(i, carry):
        earlier = pick(lax.axis_index("ctx"), got, i)
        earlier_ref[i] = earlier
        fq = fq_ref[i]
        raw = raw_ref[i] + dot(fq, earlier, 1, 0)
        inverse = lax.rsqrt(jnp.mean(raw * raw, axis=-1, keepdims=True) + 1.0)
        normed = raw * inverse
        up = gh_ref[i].astype(F32)
        grad = inverse * (up - normed * jnp.mean(up * normed, axis=-1, keepdims=True))
        grad = grad.astype(BF)
        wide_ref[pl.ds(base + i, t, stride=heads), :] = normed
        grad_raw_ref[i] = grad
        grad_ref[i] = dot(fq, grad, 0, 0).astype(BF)
        return carry

    lax.fori_loop(0, size, one, 0, unroll=UNROLL)


def back_kernel(base, size, heads, t, fq_ref, fk_ref, vh_ref, slope_ref, score_ref, grad_raw_ref, earlier_ref, *rest):
    gk_ref, gv_ref, wide_ref = rest[-3:]

    def one(i, carry):
        grad = grad_raw_ref[i]
        fq = fq_ref[i]
        grad_scores = jnp.where(low_mask(t), dot(grad, vh_ref[i], 1, 1), 0.0).astype(BF)
        gfq = dot(grad_scores, fk_ref[i], 1, 0) + dot(grad, earlier_ref[i], 1, 1)
        wide_ref[pl.ds(base + i, t, stride=heads), :] = gfq * slope_ref[i]
        gk_ref[i] = dot(grad_scores, fq, 0, 0)
        gv_ref[i] = dot(score_ref[i], grad, 0, 0)
        return carry

    lax.fori_loop(0, size, one, 0, unroll=UNROLL)


def gather_kernel(count, *refs):
    flush(refs[:count], refs[2 * count : 3 * count], refs[count : 2 * count], refs[-1])


def later_kernel(base, size, heads, t, chain, fk_ref, vh_ref, slope_ref, gk, gv, *rest):
    got, (wide_k, wide_v) = rest[: chain.hops], rest[-2:]

    def one(i, carry):
        later = pick(chain.n - 1 - lax.axis_index("ctx"), got, i)
        gfk = gk[i] + dot(vh_ref[i], later, 1, 1)
        wide_k[pl.ds(base + i, t, stride=heads), :] = gfk * slope_ref[i]
        wide_v[pl.ds(base + i, t, stride=heads), :] = gv[i] + dot(fk_ref[i], later, 1, 0)
        return carry

    lax.fori_loop(0, size, one, 0, unroll=UNROLL)


def last_kernel(base, size, heads, t, chain, *refs):
    fk_ref, vh_ref, slope_ref, gk, gv = refs[:5]
    got = refs[5 : 5 + chain.hops]
    if base:
        wide_k, wide_v, k_out, v_out, k16, v16, sems, later_ref = refs[5 + chain.hops :]
    else:
        k_out, v_out, k16, v16, sems, later_ref, wide_k, wide_v = refs[5 + chain.hops :]
    for i in range(size):
        later_ref[i] = pick(chain.n - 1 - lax.axis_index("ctx"), got, i)
    copies = []
    count = t // BLOCKS
    for at in range(0, t, count):
        here = pl.ds(at, count)
        rows = pl.ds(at * heads, count * heads)
        for wide, stage, dst in ((wide_v, v16, v_out), (wide_k, k16, k_out)):
            for i in range(size):
                if wide is wide_v:
                    value = gv[i, here] + dot(fk_ref[i, here], later_ref[i], 1, 0)
                else:
                    value = (gk[i, here] + dot(vh_ref[i, here], later_ref[i], 1, 1)) * slope_ref[i, here]
                wide[pl.ds(at * heads + base + i, count, stride=heads), :] = value
            stage[rows, :] = wide[rows, :].astype(BF)
            copies.append(pltpu.make_async_copy(stage.at[rows], dst.at[rows], sems.at[len(copies)]))
            copies[-1].start()
    for copy in copies:
        copy.wait()


def call(body, outs, scratch, args, flops, name, specs, out_specs, aliases):
    moved = sum(a.size * a.dtype.itemsize for a in args)
    return pl.pallas_call(
        body,
        out_shape=outs,
        in_specs=specs,
        out_specs=out_specs,
        scratch_shapes=scratch,
        input_output_aliases=aliases,
        compiler_params=pltpu.CompilerParams(vmem_limit_bytes=SCOPED),
        cost_estimate=pl.CostEstimate(flops=flops, bytes_accessed=moved, transcendentals=0),
        name=name,
    )(*args)


def swap(x, low, n, cores):
    pairs = []
    for c in range(n):
        for r in range(cores):
            to = (2 * low + 1 - c, r) if c in (low, low + 1) else (c, r ^ 1 if cores % 2 == 0 else r)
            pairs.append((c * cores + r, to[0] * cores + to[1]))
    return lax.ppermute(x, ("ctx", "rep"), pairs)


class Order:
    def __init__(self):
        self.before = []

    def tie(self, x):
        return lax.optimization_barrier((x, *self.before))[0] if self.before else x

    def compute(self, body, outs, scratch, args, tied, flops, name, far_in=(), far_out=(), aliases={}):
        args = list(args)
        args[tied] = self.tie(args[tied])
        for i in far_in:
            args[i] = pltpu.with_memory_space_constraint(args[i], pltpu.HBM)
        near, far = pl.BlockSpec(memory_space=pltpu.VMEM), pl.BlockSpec(memory_space=pltpu.HBM)
        made = call(
            body, outs, scratch, args, flops, name,
            [far if i in far_in else near for i in range(len(args))],
            [far if i in far_out else near for i in range(len(outs))], aliases,
        )
        self.before = [made[0]]
        return made


class Chain:
    def __init__(self, order, part, n, cores, reverse):
        self.order, self.part, self.n, self.cores, self.reverse = order, part, n, cores, reverse
        self.got = []
        self.hops = n - 1

    def carried(self):
        if not self.got:
            return self.order.tie(self.part)
        return (self.part.astype(F32) + self.order.tie(self.got[-1]).astype(F32)).astype(BF)

    def hop(self):
        running = self.carried()
        self.order.before.append(running)
        h = len(self.got)
        self.got.append(swap(running, self.n - 2 - h if self.reverse else h, self.n, self.cores))


def merge_kernel(n, part_ref, got_ref, other_ref, out_ref):
    total = (part_ref[...].astype(F32) + got_ref[...].astype(F32)).astype(BF)
    out_ref[...] = jnp.where(lax.axis_index("ctx") == n - 1, other_ref[...], total)


def join(up, down):
    if up.part.shape != down.part.shape or not up.got:
        up.hop()
        down.hop()
        return
    running, = up.order.compute(
        functools.partial(merge_kernel, up.n), [jax.ShapeDtypeStruct(up.part.shape, BF)], [],
        (up.part, up.got[-1], down.part), 1, 3 * up.part.size, "merge",
    )
    received = swap(running, up.n - 2, up.n, up.cores)
    up.got.append(received)
    down.got.append(received)


def pick(place, got, i):
    total = jnp.zeros(got[0].shape[1:], BF)
    for hop, part in enumerate(got):
        total = jnp.where(place == hop + 1, part[i], total)
    return total


def plan(hops):
    joined = {name for step in ORDER if step[0] == "x" for name in ("u" + step[1], "d" + step[2])}
    done = dict.fromkeys(ORDER, 0)
    for step in ORDER:
        done[step] += 1
        if step[0] not in "ud":
            yield step
            continue
        wanted = hops - (step in joined)
        if done[step] == ORDER.count(step):
            yield from [step] * (wanted - done[step] + 1)
        elif done[step] <= wanted:
            yield step


def shards(n, cores, query_in, key_in, value_in, grad_out):
    _, t, heads, d = query_in.shape
    sizes = SIZES if sum(SIZES) == heads else [heads // len(SIZES)] * len(SIZES)
    assert sum(sizes) == heads
    m = len(sizes)
    bases = [sum(sizes[:c]) for c in range(m)]
    q, k, v, g = (a.reshape(t * heads, d) for a in (query_in, key_in, value_in, grad_out))
    S = jax.ShapeDtypeStruct
    flat = S((t * heads, d), BF)
    wide = pltpu.VMEM((t * heads, d), F32)
    mm = 2 * t * d * d

    order = Order()
    flat16 = pltpu.VMEM((t * heads, d), BF)
    sems = pltpu.SemaphoreType.DMA((2 * BLOCKS,))
    broad = S((t * heads, d), F32)
    up, down, parts, held = {}, {}, {}, {}

    def of(c, dt):
        return S((sizes[c], t, d), dt)

    def key(c):
        outs = [S((sizes[c], d, d), BF), of(c, BF), of(c, BF), of(c, F32)]
        body = functools.partial(key_kernel, bases[c], sizes[c], heads, t, c == 0)
        if c == 0:
            state, *held["key", c], held["k32"], held["v32"] = order.compute(
                body, outs + [broad] * 2, [flat16, flat16, sems, sems], (k, v), 0, sizes[c] * mm, "key", far_in=(0, 1)
            )
        else:
            state, *held["key", c] = order.compute(
                body, outs, [], (held["k32"], held["v32"]), 0, sizes[c] * mm, "key"
            )
        up[c] = Chain(order, state, n, cores, False)

    def query(c):
        outs = [of(c, F32), of(c, BF), of(c, BF), of(c, F32), S((sizes[c], t, t), BF)]
        fk, vh, _ = held["key", c]
        body = functools.partial(query_kernel, bases[c], sizes[c], heads, t, c == 0)
        if c == 0:
            *held["query", c], held["q32"], held["g32"] = order.compute(
                body, outs + [broad] * 2, [], (q, g, fk, vh), 2, sizes[c] * mm * 4, "query"
            )
        else:
            held["query", c] = order.compute(
                body, outs, [], (held["q32"], held["g32"], fk, vh), 2, sizes[c] * mm * 4, "query"
            )

    def onto(args, outs, names):
        have = [held[name] for name in names if name in held]
        aliases = {len(args) + i: len(outs) + i for i in range(len(have))}
        return (*args, *have), outs + [broad] * len(names), aliases

    def norm(c):
        raw, fq, gh, _, _ = held["query", c]
        s = sizes[c]
        state = S((s, d, d), BF)
        args, outs, aliases = onto((fq, gh, raw, *up[c].got), [state, S((s, t, d), BF), state], ["normed"])
        grad, grad_raw, earlier, held["normed"] = order.compute(
            functools.partial(norm_kernel, bases[c], s, heads, t, up[c]),
            outs, [], args, 3, s * mm * 2, "norm", aliases=aliases,
        )
        held[c] = grad_raw, earlier
        down[c] = Chain(order, grad, n, cores, True)

    def back(c):
        _, fq, _, slope_q, scores = held["query", c]
        fk, vh, _ = held["key", c]
        s = sizes[c]
        piece = S((s, t, d), F32)
        args, outs, aliases = onto((fq, fk, vh, slope_q, scores, *held[c]), [piece, piece], ["gq"])
        *parts[c], held["gq"] = order.compute(
            functools.partial(back_kernel, bases[c], s, heads, t),
            outs, [], args, 6, s * mm * 9, "back", aliases=aliases,
        )

    def gather(which):
        name = ("normed", "gq")[which]
        held["out", which], = order.compute(
            functools.partial(gather_kernel, 1), [flat], [flat16, sems], [held[name]], 0, heads * mm, "gather",
            far_out=(0,),
        )

    def later(c):
        s = sizes[c]
        args = (*held["key", c], *parts[c], *down[c].got)
        if c < m - 1:
            args, outs, aliases = onto(args, [], ["gk", "gv"])
            held["gk"], held["gv"] = order.compute(
                functools.partial(later_kernel, bases[c], s, heads, t, down[c]),
                outs, [], args, 5, s * mm * 2, "later", aliases=aliases,
            )
        else:
            wides = [held["gk"], held["gv"]] if m > 1 else []
            held["last"] = order.compute(
                functools.partial(last_kernel, bases[c], s, heads, t, down[c]),
                [flat, flat], [flat16, flat16, sems, pltpu.VMEM((s, d, d), BF)] + ([] if wides else [wide, wide]),
                (*args, *wides), 5, s * mm * 2, "last", far_out=(0, 1),
            )

    steps = dict(
        u=lambda c: up[c].hop(), d=lambda c: down[c].hop(), x=lambda c, e: join(up[c], down[e]),
        k=key, q=query, n=norm, b=back, g=gather, l=later,
    )
    for step in plan(n - 1):
        steps[step[0]](*map(int, step[1:]))
    output, grad_query = held["out", 0], held["out", 1]
    grad_key, grad_value = held["last"]
    return tuple(a.reshape(1, t, heads, d) for a in (output, grad_query, grad_key, grad_value))


def solution(mesh):
    placed = P(("groups", "rep"), "ctx", "head", None)
    return jax.shard_map(
        functools.partial(shards, mesh.shape["ctx"], mesh.shape["rep"]),
        mesh=mesh,
        in_specs=(placed,) * 4,
        out_specs=(placed,) * 4,
        check_vma=False,
    )
```

```python
import functools

import jax
import jax.numpy as jnp
from jax import lax
from jax.experimental import pallas as pl
from jax.experimental.pallas import tpu as pltpu
from jax.sharding import PartitionSpec as P

BF, F32 = jnp.bfloat16, jnp.float32
MIB = 1 << 20
SCOPED = 12 * MIB
SIZES = [4, 4, 4, 4]
UNROLL = 4
BLOCKS = 4
ORDER = [
    "k0", "u0", "k2", "k1", "q0", "u1", "u2", "q1", "u0", "k3", "u3", "u1", "u0", "u2",
    "q3", "u1", "u3", "n0", "x20", "q2", "n1", "x31", "b1", "d0", "n2", "d2", "d1", "n3",
    "d3", "d0", "d2", "d1", "g0", "d3", "d2", "b3", "b0", "d3", "l1", "l0", "b2", "g1",
    "l2", "l3",
]


def dot(a, b, ca, cb):
    return lax.dot_general(a, b, (((ca,), (cb,)), ((), ())), preferred_element_type=F32)


def silu_parts(x):
    sigma = 1.0 / (1.0 + jnp.exp(-x))
    return x * sigma, sigma * (1.0 + x * (1.0 - sigma))


def low_mask(t):
    rows = lax.broadcasted_iota(jnp.int32, (t, t), 0)
    cols = lax.broadcasted_iota(jnp.int32, (t, t), 1)
    return rows >= cols


def widen(src, dst):
    dst[...] = src[...].astype(F32)


def blocks_of(rows):
    size = rows // BLOCKS if rows % (16 * BLOCKS) == 0 else rows
    return [pl.ds(at, size) for at in range(0, rows, size)]


def fetch(src, landing, sems):
    copies = []
    for rows in blocks_of(src.shape[0]):
        copies.append((pltpu.make_async_copy(src.at[rows], landing.at[rows], sems.at[len(copies)]), rows))
        copies[-1][0].start()
    return copies


def land(copies, landing, wide):
    for copy, rows in copies:
        copy.wait()
        wide[rows, :] = landing[rows, :].astype(F32)


def flush(wides, stages, results, sems):
    copies = []
    for wide, stage, dst in zip(wides, stages, results):
        for rows in blocks_of(wide.shape[0]):
            stage[rows, :] = wide[rows, :].astype(BF)
            copies.append(pltpu.make_async_copy(stage.at[rows], dst.at[rows], sems.at[len(copies)]))
            copies[-1].start()
    for copy in copies:
        copy.wait()


def key_kernel(base, size, heads, t, first, *refs):
    if first:
        k_ref, v_ref, state_ref, fk_ref, vh_ref, slope_ref, k32, v32, k16, v16, k_sems, v_sems = refs
        k_copies, v_copies = fetch(k_ref, k16, k_sems), fetch(v_ref, v16, v_sems)
        land(k_copies, k16, k32)
        land(v_copies, v16, v32)
    else:
        k32, v32, state_ref, fk_ref, vh_ref, slope_ref = refs

    def one(i, carry):
        feat, slope = silu_parts(k32[pl.ds(base + i, t, stride=heads), :])
        feat = feat.astype(BF)
        vh = v32[pl.ds(base + i, t, stride=heads), :].astype(BF)
        fk_ref[i] = feat
        vh_ref[i] = vh
        slope_ref[i] = slope
        state_ref[i] = dot(feat, vh, 0, 0).astype(BF)
        return carry

    lax.fori_loop(0, size, one, 0, unroll=UNROLL)


def query_kernel(base, size, heads, t, first, *refs):
    if first:
        q_ref, g_ref, fk_ref, vh_ref, raw_ref, fq_ref, gh_ref, slope_ref, score_ref, q32, g32 = refs
        widen(q_ref, q32)
        widen(g_ref, g32)
    else:
        q32, g32, fk_ref, vh_ref, raw_ref, fq_ref, gh_ref, slope_ref, score_ref = refs

    def one(i, carry):
        feat, slope = silu_parts(q32[pl.ds(base + i, t, stride=heads), :])
        feat = feat.astype(BF)
        fq_ref[i] = feat
        slope_ref[i] = slope
        gh_ref[i] = g32[pl.ds(base + i, t, stride=heads), :].astype(BF)
        scores = jnp.where(low_mask(t), dot(feat, fk_ref[i], 1, 1), 0.0).astype(BF)
        score_ref[i] = scores
        raw_ref[i] = dot(scores, vh_ref[i], 1, 0)
        return carry

    lax.fori_loop(0, size, one, 0, unroll=UNROLL)


def norm_kernel(base, size, heads, t, chain, fq_ref, gh_ref, raw_ref, *rest):
    got, (grad_ref, grad_raw_ref, earlier_ref, wide_ref) = rest[: chain.hops], rest[-4:]

    def one(i, carry):
        earlier = pick(lax.axis_index("ctx"), got, i)
        earlier_ref[i] = earlier
        fq = fq_ref[i]
        raw = raw_ref[i] + dot(fq, earlier, 1, 0)
        inverse = lax.rsqrt(jnp.mean(raw * raw, axis=-1, keepdims=True) + 1.0)
        normed = raw * inverse
        up = gh_ref[i].astype(F32)
        grad = inverse * (up - normed * jnp.mean(up * normed, axis=-1, keepdims=True))
        grad = grad.astype(BF)
        wide_ref[pl.ds(base + i, t, stride=heads), :] = normed
        grad_raw_ref[i] = grad
        grad_ref[i] = dot(fq, grad, 0, 0).astype(BF)
        return carry

    lax.fori_loop(0, size, one, 0, unroll=UNROLL)


def back_kernel(base, size, heads, t, fq_ref, fk_ref, vh_ref, slope_ref, score_ref, grad_raw_ref, earlier_ref, *rest):
    gk_ref, gv_ref, wide_ref = rest[-3:]

    def one(i, carry):
        grad = grad_raw_ref[i]
        fq = fq_ref[i]
        grad_scores = jnp.where(low_mask(t), dot(grad, vh_ref[i], 1, 1), 0.0).astype(BF)
        gfq = dot(grad_scores, fk_ref[i], 1, 0) + dot(grad, earlier_ref[i], 1, 1)
        wide_ref[pl.ds(base + i, t, stride=heads), :] = gfq * slope_ref[i]
        gk_ref[i] = dot(grad_scores, fq, 0, 0)
        gv_ref[i] = dot(score_ref[i], grad, 0, 0)
        return carry

    lax.fori_loop(0, size, one, 0, unroll=UNROLL)


def gather_kernel(count, *refs):
    flush(refs[:count], refs[2 * count : 3 * count], refs[count : 2 * count], refs[-1])


def later_kernel(base, size, heads, t, chain, fk_ref, vh_ref, slope_ref, gk, gv, *rest):
    got, (wide_k, wide_v) = rest[: chain.hops], rest[-2:]

    def one(i, carry):
        later = pick(chain.n - 1 - lax.axis_index("ctx"), got, i)
        gfk = gk[i] + dot(vh_ref[i], later, 1, 1)
        wide_k[pl.ds(base + i, t, stride=heads), :] = gfk * slope_ref[i]
        wide_v[pl.ds(base + i, t, stride=heads), :] = gv[i] + dot(fk_ref[i], later, 1, 0)
        return carry

    lax.fori_loop(0, size, one, 0, unroll=UNROLL)


def last_kernel(base, size, heads, t, chain, *refs):
    fk_ref, vh_ref, slope_ref, gk, gv = refs[:5]
    got = refs[5 : 5 + chain.hops]
    if base:
        wide_k, wide_v, k_out, v_out, k16, v16, sems, later_ref = refs[5 + chain.hops :]
    else:
        k_out, v_out, k16, v16, sems, later_ref, wide_k, wide_v = refs[5 + chain.hops :]
    for i in range(size):
        later_ref[i] = pick(chain.n - 1 - lax.axis_index("ctx"), got, i)
    copies = []
    count = t // BLOCKS
    for at in range(0, t, count):
        here = pl.ds(at, count)
        rows = pl.ds(at * heads, count * heads)
        for wide, stage, dst in ((wide_v, v16, v_out), (wide_k, k16, k_out)):
            for i in range(size):
                if wide is wide_v:
                    value = gv[i, here] + dot(fk_ref[i, here], later_ref[i], 1, 0)
                else:
                    value = (gk[i, here] + dot(vh_ref[i, here], later_ref[i], 1, 1)) * slope_ref[i, here]
                wide[pl.ds(at * heads + base + i, count, stride=heads), :] = value
            stage[rows, :] = wide[rows, :].astype(BF)
            copies.append(pltpu.make_async_copy(stage.at[rows], dst.at[rows], sems.at[len(copies)]))
            copies[-1].start()
    for copy in copies:
        copy.wait()


def call(body, outs, scratch, args, flops, name, specs, out_specs, aliases):
    moved = sum(a.size * a.dtype.itemsize for a in args)
    return pl.pallas_call(
        body,
        out_shape=outs,
        in_specs=specs,
        out_specs=out_specs,
        scratch_shapes=scratch,
        input_output_aliases=aliases,
        compiler_params=pltpu.CompilerParams(vmem_limit_bytes=SCOPED),
        cost_estimate=pl.CostEstimate(flops=flops, bytes_accessed=moved, transcendentals=0),
        name=name,
    )(*args)


def swap(x, low, n, cores):
    pairs = []
    for c in range(n):
        for r in range(cores):
            to = (2 * low + 1 - c, r) if c in (low, low + 1) else (c, r ^ 1 if cores % 2 == 0 else r)
            pairs.append((c * cores + r, to[0] * cores + to[1]))
    return lax.ppermute(x, ("ctx", "rep"), pairs)


class Order:
    def __init__(self):
        self.before = []

    def tie(self, x):
        return lax.optimization_barrier((x, *self.before))[0] if self.before else x

    def compute(self, body, outs, scratch, args, tied, flops, name, far_in=(), far_out=(), aliases={}):
        args = list(args)
        args[tied] = self.tie(args[tied])
        for i in far_in:
            args[i] = pltpu.with_memory_space_constraint(args[i], pltpu.HBM)
        near, far = pl.BlockSpec(memory_space=pltpu.VMEM), pl.BlockSpec(memory_space=pltpu.HBM)
        made = call(
            body, outs, scratch, args, flops, name,
            [far if i in far_in else near for i in range(len(args))],
            [far if i in far_out else near for i in range(len(outs))], aliases,
        )
        self.before = [made[0]]
        return made


class Chain:
    def __init__(self, order, part, n, cores, reverse):
        self.order, self.part, self.n, self.cores, self.reverse = order, part, n, cores, reverse
        self.got = []
        self.hops = n - 1

    def carried(self):
        if not self.got:
            return self.order.tie(self.part)
        return (self.part.astype(F32) + self.order.tie(self.got[-1]).astype(F32)).astype(BF)

    def hop(self):
        running = self.carried()
        self.order.before.append(running)
        h = len(self.got)
        self.got.append(swap(running, self.n - 2 - h if self.reverse else h, self.n, self.cores))


def merge_kernel(n, part_ref, got_ref, other_ref, out_ref):
    total = (part_ref[...].astype(F32) + got_ref[...].astype(F32)).astype(BF)
    out_ref[...] = jnp.where(lax.axis_index("ctx") == n - 1, other_ref[...], total)


def join(up, down):
    if up.part.shape != down.part.shape or not up.got:
        up.hop()
        down.hop()
        return
    running, = up.order.compute(
        functools.partial(merge_kernel, up.n), [jax.ShapeDtypeStruct(up.part.shape, BF)], [],
        (up.part, up.got[-1], down.part), 1, 3 * up.part.size, "merge",
    )
    received = swap(running, up.n - 2, up.n, up.cores)
    up.got.append(received)
    down.got.append(received)


def pick(place, got, i):
    total = jnp.zeros(got[0].shape[1:], BF)
    for hop, part in enumerate(got):
        total = jnp.where(place == hop + 1, part[i], total)
    return total


def plan(hops):
    joined = {name for step in ORDER if step[0] == "x" for name in ("u" + step[1], "d" + step[2])}
    done = dict.fromkeys(ORDER, 0)
    for step in ORDER:
        done[step] += 1
        if step[0] not in "ud":
            yield step
            continue
        wanted = hops - (step in joined)
        if done[step] == ORDER.count(step):
            yield from [step] * (wanted - done[step] + 1)
        elif done[step] <= wanted:
            yield step


def shards(n, cores, query_in, key_in, value_in, grad_out):
    _, t, heads, d = query_in.shape
    sizes = SIZES if sum(SIZES) == heads else [heads // len(SIZES)] * len(SIZES)
    assert sum(sizes) == heads
    m = len(sizes)
    bases = [sum(sizes[:c]) for c in range(m)]
    q, k, v, g = (a.reshape(t * heads, d) for a in (query_in, key_in, value_in, grad_out))
    S = jax.ShapeDtypeStruct
    flat = S((t * heads, d), BF)
    wide = pltpu.VMEM((t * heads, d), F32)
    mm = 2 * t * d * d

    order = Order()
    flat16 = pltpu.VMEM((t * heads, d), BF)
    sems = pltpu.SemaphoreType.DMA((2 * BLOCKS,))
    broad = S((t * heads, d), F32)
    up, down, parts, held = {}, {}, {}, {}

    def of(c, dt):
        return S((sizes[c], t, d), dt)

    def key(c):
        outs = [S((sizes[c], d, d), BF), of(c, BF), of(c, BF), of(c, F32)]
        body = functools.partial(key_kernel, bases[c], sizes[c], heads, t, c == 0)
        if c == 0:
            state, *held["key", c], held["k32"], held["v32"] = order.compute(
                body, outs + [broad] * 2, [flat16, flat16, sems, sems], (k, v), 0, sizes[c] * mm, "key", far_in=(0, 1)
            )
        else:
            state, *held["key", c] = order.compute(
                body, outs, [], (held["k32"], held["v32"]), 0, sizes[c] * mm, "key"
            )
        up[c] = Chain(order, state, n, cores, False)

    def query(c):
        outs = [of(c, F32), of(c, BF), of(c, BF), of(c, F32), S((sizes[c], t, t), BF)]
        fk, vh, _ = held["key", c]
        body = functools.partial(query_kernel, bases[c], sizes[c], heads, t, c == 0)
        if c == 0:
            *held["query", c], held["q32"], held["g32"] = order.compute(
                body, outs + [broad] * 2, [], (q, g, fk, vh), 2, sizes[c] * mm * 4, "query"
            )
        else:
            held["query", c] = order.compute(
                body, outs, [], (held["q32"], held["g32"], fk, vh), 2, sizes[c] * mm * 4, "query"
            )

    def onto(args, outs, names):
        have = [held[name] for name in names if name in held]
        aliases = {len(args) + i: len(outs) + i for i in range(len(have))}
        return (*args, *have), outs + [broad] * len(names), aliases

    def norm(c):
        raw, fq, gh, _, _ = held["query", c]
        s = sizes[c]
        state = S((s, d, d), BF)
        args, outs, aliases = onto((fq, gh, raw, *up[c].got), [state, S((s, t, d), BF), state], ["normed"])
        grad, grad_raw, earlier, held["normed"] = order.compute(
            functools.partial(norm_kernel, bases[c], s, heads, t, up[c]),
            outs, [], args, 3, s * mm * 2, "norm", aliases=aliases,
        )
        held[c] = grad_raw, earlier
        down[c] = Chain(order, grad, n, cores, True)

    def back(c):
        _, fq, _, slope_q, scores = held["query", c]
        fk, vh, _ = held["key", c]
        s = sizes[c]
        piece = S((s, t, d), F32)
        args, outs, aliases = onto((fq, fk, vh, slope_q, scores, *held[c]), [piece, piece], ["gq"])
        *parts[c], held["gq"] = order.compute(
            functools.partial(back_kernel, bases[c], s, heads, t),
            outs, [], args, 6, s * mm * 9, "back", aliases=aliases,
        )

    def gather(which):
        name = ("normed", "gq")[which]
        held["out", which], = order.compute(
            functools.partial(gather_kernel, 1), [flat], [flat16, sems], [held[name]], 0, heads * mm, "gather",
            far_out=(0,),
        )

    def later(c):
        s = sizes[c]
        args = (*held["key", c], *parts[c], *down[c].got)
        if c < m - 1:
            args, outs, aliases = onto(args, [], ["gk", "gv"])
            held["gk"], held["gv"] = order.compute(
                functools.partial(later_kernel, bases[c], s, heads, t, down[c]),
                outs, [], args, 5, s * mm * 2, "later", aliases=aliases,
            )
        else:
            wides = [held["gk"], held["gv"]] if m > 1 else []
            held["last"] = order.compute(
                functools.partial(last_kernel, bases[c], s, heads, t, down[c]),
                [flat, flat], [flat16, flat16, sems, pltpu.VMEM((s, d, d), BF)] + ([] if wides else [wide, wide]),
                (*args, *wides), 5, s * mm * 2, "last", far_out=(0, 1),
            )

    steps = dict(
        u=lambda c: up[c].hop(), d=lambda c: down[c].hop(), x=lambda c, e: join(up[c], down[e]),
        k=key, q=query, n=norm, b=back, g=gather, l=later,
    )
    for step in plan(n - 1):
        steps[step[0]](*map(int, step[1:]))
    output, grad_query = held["out", 0], held["out", 1]
    grad_key, grad_value = held["last"]
    return tuple(a.reshape(1, t, heads, d) for a in (output, grad_query, grad_key, grad_value))


def solution(mesh):
    placed = P(("groups", "rep"), "ctx", "head", None)
    return jax.shard_map(
        functools.partial(shards, mesh.shape["ctx"], mesh.shape["rep"]),
        mesh=mesh,
        in_specs=(placed,) * 4,
        out_specs=(placed,) * 4,
        check_vma=False,
    )
```

```python
import functools

import jax
import jax.numpy as jnp
from jax import lax
from jax.experimental import pallas as pl
from jax.experimental.pallas import tpu as pltpu
from jax.sharding import PartitionSpec as P

BF, F32 = jnp.bfloat16, jnp.float32
MIB = 1 << 20
SCOPED = 12 * MIB
SIZES = [4, 4, 4, 4]
UNROLL = 4
BLOCKS = 2
ORDER = [
    "k0", "u0", "k2", "k1", "q0", "u1", "u2", "q1", "u0", "k3", "u3", "u1", "u0", "u2",
    "q3", "u1", "u3", "n0", "x20", "q2", "n1", "x31", "b1", "d0", "n2", "d2", "d1", "n3",
    "d3", "d0", "d2", "d1", "g0", "d3", "d2", "b3", "b0", "d3", "l1", "l0", "b2", "g1",
    "l2", "l3",
]


def dot(a, b, ca, cb):
    return lax.dot_general(a, b, (((ca,), (cb,)), ((), ())), preferred_element_type=F32)


def silu_parts(x):
    sigma = 1.0 / (1.0 + jnp.exp(-x))
    return x * sigma, sigma * (1.0 + x * (1.0 - sigma))


def low_mask(t):
    rows = lax.broadcasted_iota(jnp.int32, (t, t), 0)
    cols = lax.broadcasted_iota(jnp.int32, (t, t), 1)
    return rows >= cols


def widen(src, dst):
    dst[...] = src[...].astype(F32)


def blocks_of(rows):
    size = rows // BLOCKS if rows % (16 * BLOCKS) == 0 else rows
    return [pl.ds(at, size) for at in range(0, rows, size)]


def fetch(src, landing, sems):
    copies = []
    for rows in blocks_of(src.shape[0]):
        copies.append((pltpu.make_async_copy(src.at[rows], landing.at[rows], sems.at[len(copies)]), rows))
        copies[-1][0].start()
    return copies


def land(copies, landing, wide):
    for copy, rows in copies:
        copy.wait()
        wide[rows, :] = landing[rows, :].astype(F32)


def flush(wides, stages, results, sems):
    copies = []
    for wide, stage, dst in zip(wides, stages, results):
        for rows in blocks_of(wide.shape[0]):
            stage[rows, :] = wide[rows, :].astype(BF)
            copies.append(pltpu.make_async_copy(stage.at[rows], dst.at[rows], sems.at[len(copies)]))
            copies[-1].start()
    for copy in copies:
        copy.wait()


def key_kernel(base, size, heads, t, first, *refs):
    if first:
        k_ref, v_ref, state_ref, fk_ref, vh_ref, slope_ref, k32, v32, k16, v16, k_sems, v_sems = refs
        k_copies, v_copies = fetch(k_ref, k16, k_sems), fetch(v_ref, v16, v_sems)
        land(k_copies, k16, k32)
        land(v_copies, v16, v32)
    else:
        k32, v32, state_ref, fk_ref, vh_ref, slope_ref = refs

    def one(i, carry):
        feat, slope = silu_parts(k32[pl.ds(base + i, t, stride=heads), :])
        feat = feat.astype(BF)
        vh = v32[pl.ds(base + i, t, stride=heads), :].astype(BF)
        fk_ref[i] = feat
        vh_ref[i] = vh
        slope_ref[i] = slope
        state_ref[i] = dot(feat, vh, 0, 0).astype(BF)
        return carry

    lax.fori_loop(0, size, one, 0, unroll=UNROLL)


def query_kernel(base, size, heads, t, first, *refs):
    if first:
        q_ref, g_ref, fk_ref, vh_ref, raw_ref, fq_ref, gh_ref, slope_ref, score_ref, q32, g32 = refs
        widen(q_ref, q32)
        widen(g_ref, g32)
    else:
        q32, g32, fk_ref, vh_ref, raw_ref, fq_ref, gh_ref, slope_ref, score_ref = refs

    def one(i, carry):
        feat, slope = silu_parts(q32[pl.ds(base + i, t, stride=heads), :])
        feat = feat.astype(BF)
        fq_ref[i] = feat
        slope_ref[i] = slope
        gh_ref[i] = g32[pl.ds(base + i, t, stride=heads), :].astype(BF)
        scores = jnp.where(low_mask(t), dot(feat, fk_ref[i], 1, 1), 0.0).astype(BF)
        score_ref[i] = scores
        raw_ref[i] = dot(scores, vh_ref[i], 1, 0)
        return carry

    lax.fori_loop(0, size, one, 0, unroll=UNROLL)


def norm_kernel(base, size, heads, t, chain, fq_ref, gh_ref, raw_ref, *rest):
    got, (grad_ref, grad_raw_ref, earlier_ref, wide_ref) = rest[: chain.hops], rest[-4:]

    def one(i, carry):
        earlier = pick(lax.axis_index("ctx"), got, i)
        earlier_ref[i] = earlier
        fq = fq_ref[i]
        raw = raw_ref[i] + dot(fq, earlier, 1, 0)
        inverse = lax.rsqrt(jnp.mean(raw * raw, axis=-1, keepdims=True) + 1.0)
        normed = raw * inverse
        up = gh_ref[i].astype(F32)
        grad = inverse * (up - normed * jnp.mean(up * normed, axis=-1, keepdims=True))
        grad = grad.astype(BF)
        wide_ref[pl.ds(base + i, t, stride=heads), :] = normed
        grad_raw_ref[i] = grad
        grad_ref[i] = dot(fq, grad, 0, 0).astype(BF)
        return carry

    lax.fori_loop(0, size, one, 0, unroll=UNROLL)


def back_kernel(base, size, heads, t, fq_ref, fk_ref, vh_ref, slope_ref, score_ref, grad_raw_ref, earlier_ref, *rest):
    gk_ref, gv_ref, wide_ref = rest[-3:]

    def one(i, carry):
        grad = grad_raw_ref[i]
        fq = fq_ref[i]
        grad_scores = jnp.where(low_mask(t), dot(grad, vh_ref[i], 1, 1), 0.0).astype(BF)
        gfq = dot(grad_scores, fk_ref[i], 1, 0) + dot(grad, earlier_ref[i], 1, 1)
        wide_ref[pl.ds(base + i, t, stride=heads), :] = gfq * slope_ref[i]
        gk_ref[i] = dot(grad_scores, fq, 0, 0)
        gv_ref[i] = dot(score_ref[i], grad, 0, 0)
        return carry

    lax.fori_loop(0, size, one, 0, unroll=UNROLL)


def gather_kernel(count, *refs):
    flush(refs[:count], refs[2 * count : 3 * count], refs[count : 2 * count], refs[-1])


def later_kernel(base, size, heads, t, chain, fk_ref, vh_ref, slope_ref, gk, gv, *rest):
    got, (wide_k, wide_v) = rest[: chain.hops], rest[-2:]

    def one(i, carry):
        later = pick(chain.n - 1 - lax.axis_index("ctx"), got, i)
        gfk = gk[i] + dot(vh_ref[i], later, 1, 1)
        wide_k[pl.ds(base + i, t, stride=heads), :] = gfk * slope_ref[i]
        wide_v[pl.ds(base + i, t, stride=heads), :] = gv[i] + dot(fk_ref[i], later, 1, 0)
        return carry

    lax.fori_loop(0, size, one, 0, unroll=UNROLL)


def last_kernel(base, size, heads, t, chain, *refs):
    fk_ref, vh_ref, slope_ref, gk, gv = refs[:5]
    got = refs[5 : 5 + chain.hops]
    if base:
        wide_k, wide_v, k_out, v_out, k16, v16, sems, later_ref = refs[5 + chain.hops :]
    else:
        k_out, v_out, k16, v16, sems, later_ref, wide_k, wide_v = refs[5 + chain.hops :]
    for i in range(size):
        later_ref[i] = pick(chain.n - 1 - lax.axis_index("ctx"), got, i)
    copies = []
    count = t // BLOCKS
    for at in range(0, t, count):
        here = pl.ds(at, count)
        rows = pl.ds(at * heads, count * heads)
        for wide, stage, dst in ((wide_v, v16, v_out), (wide_k, k16, k_out)):
            for i in range(size):
                if wide is wide_v:
                    value = gv[i, here] + dot(fk_ref[i, here], later_ref[i], 1, 0)
                else:
                    value = (gk[i, here] + dot(vh_ref[i, here], later_ref[i], 1, 1)) * slope_ref[i, here]
                wide[pl.ds(at * heads + base + i, count, stride=heads), :] = value
            stage[rows, :] = wide[rows, :].astype(BF)
            copies.append(pltpu.make_async_copy(stage.at[rows], dst.at[rows], sems.at[len(copies)]))
            copies[-1].start()
    for copy in copies:
        copy.wait()


def call(body, outs, scratch, args, flops, name, specs, out_specs, aliases):
    moved = sum(a.size * a.dtype.itemsize for a in args)
    return pl.pallas_call(
        body,
        out_shape=outs,
        in_specs=specs,
        out_specs=out_specs,
        scratch_shapes=scratch,
        input_output_aliases=aliases,
        compiler_params=pltpu.CompilerParams(vmem_limit_bytes=SCOPED),
        cost_estimate=pl.CostEstimate(flops=flops, bytes_accessed=moved, transcendentals=0),
        name=name,
    )(*args)


def swap(x, low, n, cores):
    pairs = []
    for c in range(n):
        for r in range(cores):
            to = (2 * low + 1 - c, r) if c in (low, low + 1) else (c, r ^ 1 if cores % 2 == 0 else r)
            pairs.append((c * cores + r, to[0] * cores + to[1]))
    return lax.ppermute(x, ("ctx", "rep"), pairs)


class Order:
    def __init__(self):
        self.before = []

    def tie(self, x):
        return lax.optimization_barrier((x, *self.before))[0] if self.before else x

    def compute(self, body, outs, scratch, args, tied, flops, name, far_in=(), far_out=(), aliases={}):
        args = list(args)
        args[tied] = self.tie(args[tied])
        for i in far_in:
            args[i] = pltpu.with_memory_space_constraint(args[i], pltpu.HBM)
        near, far = pl.BlockSpec(memory_space=pltpu.VMEM), pl.BlockSpec(memory_space=pltpu.HBM)
        made = call(
            body, outs, scratch, args, flops, name,
            [far if i in far_in else near for i in range(len(args))],
            [far if i in far_out else near for i in range(len(outs))], aliases,
        )
        self.before = [made[0]]
        return made


class Chain:
    def __init__(self, order, part, n, cores, reverse):
        self.order, self.part, self.n, self.cores, self.reverse = order, part, n, cores, reverse
        self.got = []
        self.hops = n - 1

    def carried(self):
        if not self.got:
            return self.order.tie(self.part)
        return (self.part.astype(F32) + self.order.tie(self.got[-1]).astype(F32)).astype(BF)

    def hop(self):
        running = self.carried()
        self.order.before.append(running)
        h = len(self.got)
        self.got.append(swap(running, self.n - 2 - h if self.reverse else h, self.n, self.cores))


def merge_kernel(n, part_ref, got_ref, other_ref, out_ref):
    total = (part_ref[...].astype(F32) + got_ref[...].astype(F32)).astype(BF)
    out_ref[...] = jnp.where(lax.axis_index("ctx") == n - 1, other_ref[...], total)


def join(up, down):
    if up.part.shape != down.part.shape or not up.got:
        up.hop()
        down.hop()
        return
    running, = up.order.compute(
        functools.partial(merge_kernel, up.n), [jax.ShapeDtypeStruct(up.part.shape, BF)], [],
        (up.part, up.got[-1], down.part), 1, 3 * up.part.size, "merge",
    )
    received = swap(running, up.n - 2, up.n, up.cores)
    up.got.append(received)
    down.got.append(received)


def pick(place, got, i):
    total = jnp.zeros(got[0].shape[1:], BF)
    for hop, part in enumerate(got):
        total = jnp.where(place == hop + 1, part[i], total)
    return total


def plan(hops):
    joined = {name for step in ORDER if step[0] == "x" for name in ("u" + step[1], "d" + step[2])}
    done = dict.fromkeys(ORDER, 0)
    for step in ORDER:
        done[step] += 1
        if step[0] not in "ud":
            yield step
            continue
        wanted = hops - (step in joined)
        if done[step] == ORDER.count(step):
            yield from [step] * (wanted - done[step] + 1)
        elif done[step] <= wanted:
            yield step


def shards(n, cores, query_in, key_in, value_in, grad_out):
    _, t, heads, d = query_in.shape
    sizes = SIZES if sum(SIZES) == heads else [heads // len(SIZES)] * len(SIZES)
    assert sum(sizes) == heads
    m = len(sizes)
    bases = [sum(sizes[:c]) for c in range(m)]
    q, k, v, g = (a.reshape(t * heads, d) for a in (query_in, key_in, value_in, grad_out))
    S = jax.ShapeDtypeStruct
    flat = S((t * heads, d), BF)
    wide = pltpu.VMEM((t * heads, d), F32)
    mm = 2 * t * d * d

    order = Order()
    flat16 = pltpu.VMEM((t * heads, d), BF)
    sems = pltpu.SemaphoreType.DMA((2 * BLOCKS,))
    broad = S((t * heads, d), F32)
    up, down, parts, held = {}, {}, {}, {}

    def of(c, dt):
        return S((sizes[c], t, d), dt)

    def key(c):
        outs = [S((sizes[c], d, d), BF), of(c, BF), of(c, BF), of(c, F32)]
        body = functools.partial(key_kernel, bases[c], sizes[c], heads, t, c == 0)
        if c == 0:
            state, *held["key", c], held["k32"], held["v32"] = order.compute(
                body, outs + [broad] * 2, [flat16, flat16, sems, sems], (k, v), 0, sizes[c] * mm, "key", far_in=(0, 1)
            )
        else:
            state, *held["key", c] = order.compute(
                body, outs, [], (held["k32"], held["v32"]), 0, sizes[c] * mm, "key"
            )
        up[c] = Chain(order, state, n, cores, False)

    def query(c):
        outs = [of(c, F32), of(c, BF), of(c, BF), of(c, F32), S((sizes[c], t, t), BF)]
        fk, vh, _ = held["key", c]
        body = functools.partial(query_kernel, bases[c], sizes[c], heads, t, c == 0)
        if c == 0:
            *held["query", c], held["q32"], held["g32"] = order.compute(
                body, outs + [broad] * 2, [], (q, g, fk, vh), 2, sizes[c] * mm * 4, "query"
            )
        else:
            held["query", c] = order.compute(
                body, outs, [], (held["q32"], held["g32"], fk, vh), 2, sizes[c] * mm * 4, "query"
            )

    def onto(args, outs, names):
        have = [held[name] for name in names if name in held]
        aliases = {len(args) + i: len(outs) + i for i in range(len(have))}
        return (*args, *have), outs + [broad] * len(names), aliases

    def norm(c):
        raw, fq, gh, _, _ = held["query", c]
        s = sizes[c]
        state = S((s, d, d), BF)
        args, outs, aliases = onto((fq, gh, raw, *up[c].got), [state, S((s, t, d), BF), state], ["normed"])
        grad, grad_raw, earlier, held["normed"] = order.compute(
            functools.partial(norm_kernel, bases[c], s, heads, t, up[c]),
            outs, [], args, 3, s * mm * 2, "norm", aliases=aliases,
        )
        held[c] = grad_raw, earlier
        down[c] = Chain(order, grad, n, cores, True)

    def back(c):
        _, fq, _, slope_q, scores = held["query", c]
        fk, vh, _ = held["key", c]
        s = sizes[c]
        piece = S((s, t, d), F32)
        args, outs, aliases = onto((fq, fk, vh, slope_q, scores, *held[c]), [piece, piece], ["gq"])
        *parts[c], held["gq"] = order.compute(
            functools.partial(back_kernel, bases[c], s, heads, t),
            outs, [], args, 6, s * mm * 9, "back", aliases=aliases,
        )

    def gather(which):
        name = ("normed", "gq")[which]
        held["out", which], = order.compute(
            functools.partial(gather_kernel, 1), [flat], [flat16, sems], [held[name]], 0, heads * mm, "gather",
            far_out=(0,),
        )

    def later(c):
        s = sizes[c]
        args = (*held["key", c], *parts[c], *down[c].got)
        if c < m - 1:
            args, outs, aliases = onto(args, [], ["gk", "gv"])
            held["gk"], held["gv"] = order.compute(
                functools.partial(later_kernel, bases[c], s, heads, t, down[c]),
                outs, [], args, 5, s * mm * 2, "later", aliases=aliases,
            )
        else:
            wides = [held["gk"], held["gv"]] if m > 1 else []
            held["last"] = order.compute(
                functools.partial(last_kernel, bases[c], s, heads, t, down[c]),
                [flat, flat], [flat16, flat16, sems, pltpu.VMEM((s, d, d), BF)] + ([] if wides else [wide, wide]),
                (*args, *wides), 5, s * mm * 2, "last", far_out=(0, 1),
            )

    steps = dict(
        u=lambda c: up[c].hop(), d=lambda c: down[c].hop(), x=lambda c, e: join(up[c], down[e]),
        k=key, q=query, n=norm, b=back, g=gather, l=later,
    )
    for step in plan(n - 1):
        steps[step[0]](*map(int, step[1:]))
    output, grad_query = held["out", 0], held["out", 1]
    grad_key, grad_value = held["last"]
    return tuple(a.reshape(1, t, heads, d) for a in (output, grad_query, grad_key, grad_value))


def solution(mesh):
    placed = P(("groups", "rep"), "ctx", "head", None)
    return jax.shard_map(
        functools.partial(shards, mesh.shape["ctx"], mesh.shape["rep"]),
        mesh=mesh,
        in_specs=(placed,) * 4,
        out_specs=(placed,) * 4,
        check_vma=False,
    )
```
